512 devices in a mesh: group: 32 (over z, x), tensor: 16 (over y, core).
Axes of the slice: x: 4, y: 8, z: 8, core: 2. Of those that a mesh axis runs over, the one named last changes fastest.
Arguments:
- tokens: bfloat16 [16384, 8192], P('group', 'tensor'), may hold values from -6 to 6
- token_slot_index: int32 [16384], P('group'), may hold values from 0 to 15
- group_slot_adapters: int32 [32, 16], replicated, may hold values from 0 to 511, as said below
- adapter_storage_position: int32 [512], replicated, may hold values from 0 to 511, as said below
- query_weight: bfloat16 [8192, 4096], P(None, 'tensor'), may hold values from -0.0625 to 0.0625
- down_weight: bfloat16 [512, 16, 8192], P(('group', 'tensor')), may hold values from -0.0625 to 0.0625
- up_weight: bfloat16 [512, 16, 4096], P(('group', 'tensor')), may hold values from -1.5 to 1.5
Outputs:
- queries: bfloat16 [16384, 4096], P('group', 'tensor')
The draws below stay inside these ranges and needn't reach their ends.
Inputs may be any that keep to these rules, and one draw needn't show every extreme that they name: `group_slot_adapters`: each row names 16 different adapters. Positions are grouped in blocks of 16 consecutive ones; at most 1 adapters of one row have positions in one block, and in every row some block holds exactly 1. `adapter_storage_position`: A permutation.
All inputs are finite; a program needn't handle non-finite values.
Results may differ from the reference program's by a relative error of at most 0.0029.
Values may be sent and summed in bfloat16 or wider, within the bound.
A program may use at most 64 MiB of HBM per device.

```python
import math
import jax
import jax.numpy as jnp
import numpy as np
from jax import lax

MODEL_WIDTH = 8192
QUERY_WIDTH = 4096
ADAPTER_RANK = 16
GROUP_SLOTS = 16
ADP_DEV = 1
TOK_GRP = 512
CAP = 1
TOKENS = 16384
ADAPTER_TOTAL = 512
N_GROUP = 32
N_TENSOR = 16


def shared_positions(key):
    resident_count = N_TENSOR * ADP_DEV
    block_count = (GROUP_SLOTS + CAP - 1) // CAP
    hot_owner = jax.random.randint(jax.random.fold_in(key, 11), (N_GROUP,), 0, 24)
    hot_local = jax.random.randint(jax.random.fold_in(key, 12), (resident_count,), 0, 24)
    spots = jnp.arange(GROUP_SLOTS, dtype=jnp.int32)
    block_index = spots // CAP
    rank_index = spots % CAP

    def one_row(row_key):
        owner_key, local_key = jax.random.split(row_key, 2)
        owner_score = (jax.random.randint(owner_key, (N_GROUP,), 0, 32) - hot_owner + 64) * N_GROUP + jnp.arange(N_GROUP, dtype=jnp.int32)
        owner_order = jnp.argsort(owner_score)[:block_count].astype(jnp.int32)
        local_score = (jax.random.randint(local_key, (block_count, resident_count), 0, 32) - hot_local[None, :] + 64) * resident_count + jnp.arange(resident_count, dtype=jnp.int32)[None, :]
        local_order = jnp.argsort(local_score, axis=1).astype(jnp.int32)
        return owner_order[block_index] * resident_count + local_order[block_index, rank_index]
    positions = jax.vmap(one_row)(jax.random.split(jax.random.fold_in(key, 13), N_GROUP))
    ordering = jax.random.permutation(jax.random.fold_in(key, 5), ADAPTER_TOTAL).astype(jnp.int32)
    return (positions, ordering)


def draw_group_slot_adapters(key, part):
    positions, ordering = shared_positions(key)
    inverse = jnp.argsort(ordering).astype(jnp.int32)
    return inverse[positions].astype(jnp.int32)


def draw_adapter_storage_position(key, part):
    positions, ordering = shared_positions(key)
    return ordering


def touch_ends(values, own_key, low, top_value):
    longest = values.shape.index(max(values.shape))
    spots = []
    for shift in (0, 1):
        where = [jax.random.randint(jax.random.fold_in(own_key, axis), (), 0, length) for axis, length in enumerate(values.shape)]
        where[longest] = (where[longest] + shift) % values.shape[longest]
        spots.append(tuple(where))
    return values.at[spots[0]].set(low).at[spots[1]].set(top_value)


def block_levels(rng, dims, cuts, smallest, largest):
    def one(position, parts):
        draws = jax.random.uniform(jax.random.fold_in(jax.random.fold_in(rng, 6), position), (parts,), jnp.float32, smallest / len(cuts), largest / len(cuts))
        return jnp.repeat(jnp.exp(draws), dims[position] // parts).reshape((-1,) + (1,) * (len(dims) - position - 1))

    level = one(*cuts[0])
    for cut in cuts[1:]:
        level = level * one(*cut)
    return level


def rank_table(count, lean):
    portions = [(1 << 20) // math.isqrt(rank ** lean) + 1 for rank in range(1, count + 1)]
    deviation = 1 + sum(portions) // (1 << 30)
    return np.cumsum(np.array([max(1, weight // deviation) for weight in portions]))


def ranked(rng, extent, amount, lean):
    table = rank_table(amount, lean)
    ticket = jax.random.randint(jax.random.fold_in(rng, 1), extent, 0, int(table[amount - 1]))
    grade = jnp.searchsorted(jnp.asarray(table, jnp.int32), ticket, side="right")
    return jax.random.permutation(jax.random.fold_in(rng, 2), amount)[grade].astype(jnp.int32)


def noise(own_key, dims, spread, most, pieces=(), kind=jnp.bfloat16):
    entries = jax.random.normal(own_key, dims, jnp.float32) * spread
    if len(pieces) > 0:
        entries = block_levels(own_key, dims, pieces, -0.22, 0.18) * entries
    return jnp.clip(entries, min=-most, max=most).astype(kind)


def setup_inputs(seed: int = 0) -> dict:
    arg_keys = jax.random.split(jax.random.key(seed), 8)
    return {
        "tokens": noise(arg_keys[0], (TOKENS, MODEL_WIDTH), 1.0, 6.0, ((0, 32), (1, 16))),
        "token_slot_index": touch_ends(ranked(arg_keys[1], (TOKENS,), GROUP_SLOTS, 2), jax.random.fold_in(arg_keys[1], 3), 0, GROUP_SLOTS - 1).astype(jnp.int32),
        "group_slot_adapters": draw_group_slot_adapters(jax.random.fold_in(arg_keys[7], 71), 0),
        "adapter_storage_position": draw_adapter_storage_position(jax.random.fold_in(arg_keys[7], 71), 0),
        "query_weight": noise(arg_keys[4], (MODEL_WIDTH, QUERY_WIDTH), MODEL_WIDTH ** -0.5, 0.0625, ((1, 16),)),
        "down_weight": noise(arg_keys[5], (ADAPTER_TOTAL, ADAPTER_RANK, MODEL_WIDTH), MODEL_WIDTH ** -0.5, 0.0625, ((0, 512),)),
        "up_weight": noise(arg_keys[6], (ADAPTER_TOTAL, ADAPTER_RANK, QUERY_WIDTH), ADAPTER_RANK ** -0.5, 1.5, ((0, 512),)),
    }


ADAPTER_SCALE = 0.5


def reference(tokens, token_slot_index, group_slot_adapters, adapter_storage_position, query_weight, down_weight, up_weight):
    slot_grid = jnp.arange(GROUP_SLOTS, dtype=jnp.int32)

    def one_group(index):
        row_block = lax.dynamic_slice_in_dim(tokens, index * TOK_GRP, TOK_GRP, 0)
        slot_rows = lax.dynamic_slice_in_dim(token_slot_index, index * TOK_GRP, TOK_GRP, 0)
        table_row = lax.dynamic_index_in_dim(group_slot_adapters, index, 0, keepdims=False)
        storage_places = adapter_storage_position[table_row]
        down_panel = down_weight[storage_places].reshape(GROUP_SLOTS * ADAPTER_RANK, MODEL_WIDTH)
        up_panel = up_weight[storage_places].reshape(GROUP_SLOTS * ADAPTER_RANK, QUERY_WIDTH)
        base_contribution = jnp.dot(row_block, query_weight, preferred_element_type=jnp.float32)
        all_slots = lax.dot_general(row_block, down_panel, (((1,), (1,)), ((), ())), preferred_element_type=jnp.float32)
        choose = (slot_rows[:, None] == slot_grid[None, :])
        shrink = jnp.sum(all_slots.reshape(TOK_GRP, GROUP_SLOTS, ADAPTER_RANK) * choose.astype(jnp.float32)[:, :, None], axis=1)
        low_rank = shrink.astype(jnp.bfloat16)
        spread_rows = (choose.astype(jnp.bfloat16)[:, :, None] * low_rank[:, None, :]).reshape(TOK_GRP, GROUP_SLOTS * ADAPTER_RANK)
        adapter_contribution = jnp.dot(spread_rows, up_panel, preferred_element_type=jnp.float32)
        return (base_contribution + ADAPTER_SCALE * adapter_contribution).astype(jnp.bfloat16)

    result = lax.map(one_group, jnp.arange(N_GROUP, dtype=jnp.int32))
    return result.reshape(TOKENS, QUERY_WIDTH)
```

```python
import functools

import jax
import jax.numpy as jnp
from jax import lax
from jax.experimental import pallas as pl
from jax.experimental.pallas import tpu as pltpu
from jax.sharding import PartitionSpec as P

RANK = 16
SLOTS = 16
SCALE = 0.5
NZ, NX, NY, NC = 8, 4, 8, 2
NG, NT = NZ * NX, NY * NC
ROWS = 512
KB = 512
NB = 256
CH = 4
CR = ROWS // CH
MESH = pl.DeviceIdType.MESH


def kernel(
    gsa, asp, idx_ref, tok, w_hbm, down, up, out_ref,
    xall, w_v, panel, staged, inbox, slots, acc, part, rs, lr, lr2, local_of,
    w_sem, x_sem, own_sem,
    ya_send, ya_recv, ga_send, ga_recv,
    ring_send, ring_recv, cross_send, cross_recv,
    rs_send, rs_recv, lr_send, lr_recv,
):
    g = lax.axis_index("group")
    t = lax.axis_index("tensor")
    y = t // NC
    c = t % NC
    other = y * NC + (1 - c)

    def tensor_peer(i):
        return lax.rem(t + i, NT)

    def group_peer(j):
        return lax.rem(g + j, NG)

    barrier = pltpu.get_barrier_semaphore()

    @pl.loop(1, NT)
    def _(i):
        pl.semaphore_signal(barrier, inc=1, device_id={"group": g, "tensor": tensor_peer(i)}, device_id_type=MESH)

    @pl.loop(1, NG)
    def _(j):
        pl.semaphore_signal(barrier, inc=1, device_id={"group": group_peer(j), "tensor": t}, device_id_type=MESH)

    w_copy = pltpu.make_async_copy(w_hbm, w_v, w_sem)
    x_copy = pltpu.make_async_copy(tok, xall.at[t], x_sem)
    down_own = pltpu.make_async_copy(
        down.at[0, :, pl.ds(pl.multiple_of(t * KB, KB), KB)], panel.at[t, :, 0:KB], own_sem.at[0])
    up_own = pltpu.make_async_copy(
        up.at[0, :, pl.ds(pl.multiple_of(t * NB, NB), NB)], panel.at[t, :, KB:KB + NB], own_sem.at[1])
    down_own.start()
    up_own.start()
    x_copy.start()
    w_copy.start()

    pl.semaphore_wait(barrier, NT - 1 + NG - 1)

    def ya_copies(i):
        dst = tensor_peer(i)
        dev = {"group": g, "tensor": dst}
        return (
            pltpu.make_async_remote_copy(
                down.at[0, :, pl.ds(pl.multiple_of(dst * KB, KB), KB)], panel.at[t, :, 0:KB],
                ya_send.at[i], ya_recv.at[i], device_id=dev, device_id_type=MESH),
            pltpu.make_async_remote_copy(
                up.at[0, :, pl.ds(pl.multiple_of(dst * NB, NB), NB)], panel.at[t, :, KB:KB + NB],
                ya_send.at[i], ya_recv.at[i], device_id=dev, device_id_type=MESH),
        )

    @pl.loop(1, NT)
    def _(i):
        a, b = ya_copies(i)
        a.start()
        b.start()

    def ring_copy(src, block, d, k, way):
        dst_y = lax.rem(y + (1 if way == 0 else NY - 1), NY)
        rows = slice(k * CR, (k + 1) * CR)
        return pltpu.make_async_remote_copy(
            src.at[rows, :], xall.at[block, rows, :],
            ring_send.at[way, d - 1, k], ring_recv.at[way, d - 1, k],
            device_id={"group": g, "tensor": dst_y * NC + c}, device_id_type=MESH)

    def cross_copy(src, block, h, k):
        rows = slice(k * CR, (k + 1) * CR)
        return pltpu.make_async_remote_copy(
            src.at[rows, :], xall.at[block, rows, :],
            cross_send.at[h, k], cross_recv.at[h, k],
            device_id={"group": g, "tensor": other}, device_id_type=MESH)

    def reaches(way, d, k):
        if d < NY // 2:
            return True
        return d == NY // 2 and (k < CH // 2) == (way == 0)

    def source(way, d):
        ys = lax.rem(y + (NY - d if way == 0 else d), NY)
        return ys * NC + c, ys * NC + (1 - c)

    for k in range(CH):
        for way in (0, 1):
            ring_copy(tok, t, 1, k, way).start()
        cross_copy(tok, t, 0, k).start()

    @pl.loop(0, NG)
    def _(r):
        pick = jnp.int32(0)
        for s in range(SLOTS):
            place = asp[gsa[r, s]]
            pick = pick + jnp.where(lax.shift_right_logical(place, 4) == g, place & 15, 0)
        local_of[r] = pick

    down_own.wait()
    up_own.wait()

    @pl.loop(1, NT)
    def _(i):
        block = panel.at[lax.rem(t + NT - i, NT)]
        pltpu.make_async_remote_copy(
            block, block, ya_send.at[i], ya_recv.at[i],
            device_id={"group": g, "tensor": tensor_peer(i)}, device_id_type=MESH).wait_recv()

    def ga_copy(j):
        dst = group_peer(j)
        return pltpu.make_async_remote_copy(
            staged.at[j], inbox.at[g], ga_send.at[j], ga_recv.at[j],
            device_id={"group": dst, "tensor": t}, device_id_type=MESH)

    @pl.loop(1, NG)
    def _(j):
        staged[j] = panel[local_of[group_peer(j)]]
        ga_copy(j).start()

    inbox[g] = panel[local_of[g]]

    x_copy.wait()
    w_copy.wait()

    def weight(block):
        return w_v[pl.ds(pl.multiple_of(block * KB, KB), KB), :]

    acc[...] = jnp.dot(xall[t], weight(t), preferred_element_type=jnp.float32)

    def accumulate(block):
        acc[...] += jnp.dot(xall[block], weight(block), preferred_element_type=jnp.float32)

    def cross_wait(h, block):
        for k in range(CH):
            cross_copy(xall.at[block], block, h, k).wait_recv()

    def ring_step(d):
        for k in range(CH):
            for way in (0, 1):
                if not reaches(way, d, k):
                    continue
                block, _ = source(way, d)
                ring_copy(xall.at[block], block, d, k, way).wait_recv()
                if reaches(way, d + 1, k):
                    ring_copy(xall.at[block], block, d + 1, k, way).start()
                h = d if way == 0 or d == NY // 2 else NY - d
                cross_copy(xall.at[block], block, h, k).start()

    def blocks_at(d):
        return (0,) if d == NY // 2 else (0, 1)

    def ring_own(d):
        for way in blocks_at(d):
            accumulate(source(way, d)[0])

    def ring_cross(d):
        for way in blocks_at(d):
            h = d if way == 0 else NY - d
            block = source(way, d)[1]
            cross_wait(h, block)
            accumulate(block)

    ring_step(1)
    ring_own(1)
    cross_wait(0, other)
    accumulate(other)
    ring_step(2)
    ring_own(2)
    ring_cross(1)

    @pl.loop(1, NG)
    def _(j):
        src = lax.rem(g + NG - j, NG)
        pltpu.make_async_remote_copy(
            inbox.at[src], inbox.at[src], ga_send.at[j], ga_recv.at[j],
            device_id={"group": group_peer(j), "tensor": t}, device_id_type=MESH).wait_recv()

    for s in range(SLOTS):
        owner = lax.shift_right_logical(asp[gsa[g, s]], 4)
        slots[s * RANK:(s + 1) * RANK, :] = inbox[owner]

    idx = idx_ref[...]
    every = lax.dot_general(
        slots[:, 0:KB], xall[t], (((1,), (1,)), ((), ())), preferred_element_type=jnp.float32)
    partial = jnp.zeros((RANK, ROWS), jnp.float32)
    for s in range(SLOTS):
        partial = partial + jnp.where(idx == s, every[s * RANK:(s + 1) * RANK, :], 0.0)
    for r in range(RANK):
        part[r] = partial[r:r + 1, :]

    def rs_copy(i):
        dst = tensor_peer(i)
        return pltpu.make_async_remote_copy(
            part.at[dst], rs.at[t], rs_send.at[i], rs_recv.at[i],
            device_id={"group": g, "tensor": dst}, device_id_type=MESH)

    @pl.loop(1, NT)
    def _(i):
        rs_copy(i).start()

    rs[t] = part[t]

    ring_step(3)
    ring_own(3)

    @pl.loop(1, NT)
    def _(i):
        src = lax.rem(t + NT - i, NT)
        pltpu.make_async_remote_copy(
            rs.at[src], rs.at[src], rs_send.at[i], rs_recv.at[i],
            device_id={"group": g, "tensor": tensor_peer(i)}, device_id_type=MESH).wait_recv()

    total = rs[0]
    for i in range(1, NT):
        total = total + rs[i]
    lr[t] = total

    def lr_copy(i):
        return pltpu.make_async_remote_copy(
            lr.at[t], lr.at[t], lr_send.at[i], lr_recv.at[i],
            device_id={"group": g, "tensor": tensor_peer(i)}, device_id_type=MESH)

    @pl.loop(1, NT)
    def _(i):
        lr_copy(i).start()

    ring_cross(2)

    @pl.loop(1, NT)
    def _(i):
        block = panel.at[t]
        pltpu.make_async_remote_copy(
            block, block, ya_send.at[i], ya_recv.at[i],
            device_id={"group": g, "tensor": tensor_peer(i)}, device_id_type=MESH).wait_send()

    @pl.loop(1, NG)
    def _(j):
        ga_copy(j).wait_send()

    @pl.loop(1, NT)
    def _(i):
        rs_copy(i).wait_send()

    @pl.loop(1, NT)
    def _(i):
        src = lax.rem(t + NT - i, NT)
        pltpu.make_async_remote_copy(
            lr.at[src], lr.at[src], lr_send.at[i], lr_recv.at[i],
            device_id={"group": g, "tensor": tensor_peer(i)}, device_id_type=MESH).wait_recv()

    for r in range(RANK):
        lr2[r:r + 1, :] = lr[r]
    low = lr2[...].astype(jnp.bfloat16).astype(jnp.float32)
    spread = jnp.concatenate([jnp.where(idx == s, low, 0.0) for s in range(SLOTS)], axis=0)
    spread = jnp.transpose(spread).astype(jnp.bfloat16)
    adapter = jnp.dot(spread, slots[:, KB:KB + NB], preferred_element_type=jnp.float32)
    acc[...] += SCALE * adapter

    ring_cross(3)
    ring_step(4)
    ring_own(4)

    @pl.loop(1, NT)
    def _(i):
        lr_copy(i).wait_send()

    for k in range(CH):
        for way in (0, 1):
            for d in range(1, NY // 2 + 1):
                if reaches(way, d, k):
                    ring_copy(xall.at[t], t, d, k, way).wait_send()

    h = NY // 2
    block = source(0, h)[1]
    cross_wait(h, block)
    out_ref[...] = (acc[...] + jnp.dot(
        xall[block], weight(block), preferred_element_type=jnp.float32)).astype(out_ref.dtype)
    for k in range(CH):
        for h in range(NY):
            cross_copy(xall.at[t], t, h, k).wait_send()


def body(tokens, token_slot_index, group_slot_adapters, adapter_storage_position, query_weight, down_weight, up_weight):
    any_space = pl.BlockSpec(memory_space=pl.ANY)
    vmem = pl.BlockSpec(memory_space=pltpu.VMEM)
    smem = pl.BlockSpec(memory_space=pltpu.SMEM)
    dma = pltpu.SemaphoreType.DMA
    bf16, f32 = jnp.bfloat16, jnp.float32
    return pl.pallas_call(
        kernel,
        out_shape=jax.ShapeDtypeStruct((ROWS, NB), bf16),
        in_specs=[smem, smem, vmem, any_space, any_space, any_space, any_space],
        out_specs=vmem,
        scratch_shapes=[
            pltpu.VMEM((NT, ROWS, KB), bf16),
            pltpu.VMEM((NT * KB, NB), bf16),
            pltpu.VMEM((NT, RANK, KB + NB), bf16),
            pltpu.VMEM((NG, RANK, KB + NB), bf16),
            pltpu.VMEM((NG, RANK, KB + NB), bf16),
            pltpu.VMEM((SLOTS * RANK, KB + NB), bf16),
            pltpu.VMEM((ROWS, NB), f32),
            pltpu.VMEM((RANK, 1, ROWS), f32),
            pltpu.VMEM((NT, 1, ROWS), f32),
            pltpu.VMEM((NT, 1, ROWS), f32),
            pltpu.VMEM((RANK, ROWS), f32),
            pltpu.SMEM((NG,), jnp.int32),
            dma, dma, dma((2,)),
            dma((NT,)), dma((NT,)), dma((NG,)), dma((NG,)),
            dma((2, NY // 2, CH)), dma((2, NY // 2, CH)), dma((NY, CH)), dma((NY, CH)),
            dma((NT,)), dma((NT,)), dma((NT,)), dma((NT,)),
        ],
        compiler_params=pltpu.CompilerParams(
            collective_id=0, has_side_effects=True, vmem_limit_bytes=48 * 1024 * 1024),
        cost_estimate=pl.CostEstimate(flops=2 * ROWS * NT * KB * NB, bytes_accessed=8 << 20, transcendentals=0),
    )(group_slot_adapters, adapter_storage_position, token_slot_index.reshape(1, ROWS),
      tokens, query_weight, down_weight, up_weight)


def solution(mesh):
    in_specs = (
        P("group", "tensor"),
        P("group"),
        P(),
        P(),
        P(None, "tensor"),
        P(("group", "tensor"), None, None),
        P(("group", "tensor"), None, None),
    )
    return jax.shard_map(body, mesh=mesh, in_specs=in_specs, out_specs=P("group", "tensor"), check_vma=False)
```

```python
import functools

import jax
import jax.numpy as jnp
from jax import lax
from jax.experimental import pallas as pl
from jax.experimental.pallas import tpu as pltpu
from jax.sharding import PartitionSpec as P

RANK = 16
SLOTS = 16
SCALE = 0.5
NZ, NX, NY, NC = 8, 4, 8, 2
NG, NT = NZ * NX, NY * NC
ROWS = 512
KB = 512
NB = 256
CH = 4
CR = ROWS // CH
VLIM = 60 * 1024
PLUS = (0, 2)
MESH = pl.DeviceIdType.MESH


def kernel(
    gsa_hbm, asp_hbm, idx_hbm, tok, w_hbm, down, up, out_ref,
    gsa, asp, idx_ref, xall, w_v, down_panel, up_panel, down_staged, up_staged, down_inbox, up_inbox, down_slots, up_slots, acc, part, rs, lr, lr2, local_of, here, opened,
    w_sem, x_sem, own_sem, table_sem,
    ya_send, ya_recv, ga_send, ga_recv,
    ring_send, ring_recv, cross_send, cross_recv,
    rs_send, rs_recv, lr_send, lr_recv,
):
    g = lax.axis_index("group")
    t = lax.axis_index("tensor")
    y = t // NC
    c = t % NC
    other = y * NC + (1 - c)

    def tensor_peer(i):
        return lax.rem(t + i, NT)

    def group_peer(j):
        return lax.rem(g + j, NG)

    barrier = pltpu.get_barrier_semaphore()

    @pl.loop(1, NT)
    def _(i):
        dst = tensor_peer(i)

        @pl.when(dst != 0)
        def _():
            pl.semaphore_signal(barrier, inc=1, device_id={"group": g, "tensor": dst}, device_id_type=MESH)

    w_copy = pltpu.make_async_copy(w_hbm, w_v, w_sem)
    x_copy = pltpu.make_async_copy(tok, xall.at[t], x_sem)
    down_own = pltpu.make_async_copy(
        down.at[0, :, pl.ds(pl.multiple_of(t * KB, KB), KB)], down_panel.at[t], own_sem.at[0])
    up_own = pltpu.make_async_copy(
        up.at[0, :, pl.ds(pl.multiple_of(t * NB, NB), NB)], up_panel.at[t], own_sem.at[1])
    tables = [
        pltpu.make_async_copy(src, dst, table_sem.at[n])
        for n, (src, dst) in enumerate(((gsa_hbm, gsa), (asp_hbm, asp), (idx_hbm, idx_ref)))
    ]
    for copy in tables:
        copy.start()
    down_own.start()
    up_own.start()
    x_copy.start()
    w_copy.start()

    @pl.when(t != 0)
    def _():
        pl.semaphore_wait(barrier, NT - 1)

    @pl.when(t == 1)
    def _():
        pl.semaphore_signal(here, inc=1, device_id={"group": g, "tensor": t - 1}, device_id_type=MESH)

    @pl.when(t == 0)
    def _():
        pl.semaphore_wait(here, 1)

    maps = (
        (down, KB, down_panel, down_staged, down_inbox, down_slots),
        (up, NB, up_panel, up_staged, up_inbox, up_slots),
    )

    def ya_copy(i, m):
        ref, width, panel = maps[m][:3]
        dst = tensor_peer(i)
        return pltpu.make_async_remote_copy(
            ref.at[0, :, pl.ds(pl.multiple_of(dst * width, width), width)], panel.at[t],
            ya_send.at[m, i], ya_recv.at[m, i], device_id={"group": g, "tensor": dst}, device_id_type=MESH)

    def ya_start(m):
        @pl.loop(1, NT)
        def _(i):
            ya_copy(i, m).start()

    def ya_landed(i, m):
        block = maps[m][2].at[lax.rem(t + NT - i, NT)]
        return pltpu.make_async_remote_copy(
            block, block, ya_send.at[m, i], ya_recv.at[m, i],
            device_id={"group": g, "tensor": tensor_peer(i)}, device_id_type=MESH)

    def ring_copy(src, block, d, k, way):
        dst_y = lax.rem(y + (1 if way == 0 else NY - 1), NY)
        rows = slice(k * CR, (k + 1) * CR)
        return pltpu.make_async_remote_copy(
            src.at[rows, :], xall.at[block, rows, :],
            ring_send.at[way, d - 1, k], ring_recv.at[way, d - 1, k],
            device_id={"group": g, "tensor": dst_y * NC + c}, device_id_type=MESH)

    def cross_copy(src, block, h, k):
        rows = slice(k * CR, (k + 1) * CR)
        return pltpu.make_async_remote_copy(
            src.at[rows, :], xall.at[block, rows, :],
            cross_send.at[h, k], cross_recv.at[h, k],
            device_id={"group": g, "tensor": other}, device_id_type=MESH)

    def reaches(way, d, k):
        if d < NY // 2:
            return True
        return d == NY // 2 and (k in PLUS) == (way == 0)

    def source(way, d):
        ys = lax.rem(y + (NY - d if way == 0 else d), NY)
        return ys * NC + c, ys * NC + (1 - c)

    def own_sends():
        for k in range(CH):
            for way in (0, 1):
                ring_copy(tok, t, 1, k, way).start()
            cross_copy(tok, t, 0, k).start()

    def greet_groups():
        @pl.when(t == 0)
        def _():
            @pl.loop(1, NG)
            def _(j):
                pl.semaphore_signal(
                    barrier, inc=1, device_id={"group": group_peer(j), "tensor": t}, device_id_type=MESH)

    def pick_adapters():
        for copy in tables:
            copy.wait()

        @pl.loop(0, NG)
        def _(r):
            pick = jnp.int32(0)
            for s in range(SLOTS):
                place = asp[gsa[s, r]]
                pick = pick + jnp.where(lax.shift_right_logical(place, 4) == g, place & 15, 0)
            local_of[r] = pick

    def panel_wait(m):
        (down_own, up_own)[m].wait()

        @pl.loop(1, NT)
        def _(i):
            ya_landed(i, m).wait_recv()

    def groups_wait():
        @pl.when(t == 0)
        def _():
            pl.semaphore_wait(barrier, NG - 1)

            @pl.loop(1, NT)
            def _(i):
                pl.semaphore_signal(
                    opened, inc=1, device_id={"group": g, "tensor": tensor_peer(i)}, device_id_type=MESH)

        @pl.when(t != 0)
        def _():
            pl.semaphore_wait(opened, 1)

    def ga_copy(j, m):
        staged, inbox = maps[m][3:5]
        dst = group_peer(j)
        return pltpu.make_async_remote_copy(
            staged.at[j], inbox.at[g],
            ga_send.at[m, j], ga_recv.at[m, j], device_id={"group": dst, "tensor": t}, device_id_type=MESH)

    def send_adapters(m):
        panel, staged, inbox = maps[m][2:5]

        @pl.loop(1, NG)
        def _(j):
            staged[j] = panel[local_of[group_peer(j)]]
            ga_copy(j, m).start()

        inbox[g] = panel[local_of[g]]

    def adapters_wait(m):
        inbox, slots = maps[m][4:]

        @pl.loop(1, NG)
        def _(j):
            block = inbox.at[lax.rem(g + NG - j, NG)]
            pltpu.make_async_remote_copy(
                block, block, ga_send.at[m, j], ga_recv.at[m, j],
                device_id={"group": group_peer(j), "tensor": t}, device_id_type=MESH).wait_recv()

        for s in range(SLOTS):
            owner = lax.shift_right_logical(asp[gsa[s, g]], 4)
            slots[s * RANK:(s + 1) * RANK, :] = inbox[owner]

    def weight(block):
        return w_v[pl.ds(pl.multiple_of(block * KB, KB), KB), :]

    def accumulate(block, first=False):
        term = jnp.dot(xall[block], weight(block), preferred_element_type=jnp.float32)
        if first:
            acc[...] = term
        else:
            acc[...] += term

    def ring_step(d, ks=range(CH)):
        for k in ks:
            for way in (0, 1):
                if not reaches(way, d, k):
                    continue
                block, _ = source(way, d)
                ring_copy(xall.at[block], block, d, k, way).wait_recv()
                if reaches(way, d + 1, k):
                    ring_copy(xall.at[block], block, d + 1, k, way).start()
                h = d if way == 0 or d == NY // 2 else NY - d
                cross_copy(xall.at[block], block, h, k).start()

    def blocks_at(d):
        return (0,) if d == NY // 2 else (0, 1)

    def ring_own(d):
        if d == 0:
            accumulate(t, True)
            return
        for way in blocks_at(d):
            accumulate(source(way, d)[0])

    def ring_cross(d):
        for way in blocks_at(d) if d else (0,):
            h = d if way == 0 else NY - d
            block = source(way, d)[1]
            for k in range(CH):
                cross_copy(xall.at[block], block, h, k).wait_recv()
            accumulate(block)

    def rs_copy(i):
        dst = tensor_peer(i)
        return pltpu.make_async_remote_copy(
            part.at[dst], rs.at[t], rs_send.at[i], rs_recv.at[i],
            device_id={"group": g, "tensor": dst}, device_id_type=MESH)

    def lr_copy(i):
        return pltpu.make_async_remote_copy(
            lr.at[t], lr.at[t], lr_send.at[i], lr_recv.at[i],
            device_id={"group": g, "tensor": tensor_peer(i)}, device_id_type=MESH)

    def shrink():
        adapters_wait(0)
        idx = idx_ref[...]
        every = lax.dot_general(
            down_slots[...], xall[t], (((1,), (1,)), ((), ())), preferred_element_type=jnp.float32)
        partial = jnp.zeros((RANK, ROWS), jnp.float32)
        for s in range(SLOTS):
            partial = partial + jnp.where(idx == s, every[s * RANK:(s + 1) * RANK, :], 0.0)
        for r in range(RANK):
            part[r] = partial[r:r + 1, :]

        @pl.loop(1, NT)
        def _(i):
            rs_copy(i).start()

        rs[t] = part[t]

    def sum_shrink():
        @pl.loop(1, NT)
        def _(i):
            src = lax.rem(t + NT - i, NT)
            pltpu.make_async_remote_copy(
                rs.at[src], rs.at[src], rs_send.at[i], rs_recv.at[i],
                device_id={"group": g, "tensor": tensor_peer(i)}, device_id_type=MESH).wait_recv()

        total = rs[0]
        for i in range(1, NT):
            total = total + rs[i]
        lr[t] = total

        @pl.loop(1, NT)
        def _(i):
            lr_copy(i).start()

    def early_sends():
        @pl.loop(1, NT)
        def _(i):
            ya_copy(i, 0).wait_send()
            ya_copy(i, 1).wait_send()
            rs_copy(i).wait_send()

        @pl.loop(1, NG)
        def _(j):
            ga_copy(j, 0).wait_send()
            ga_copy(j, 1).wait_send()

    def ring_sent(d):
        for k in range(CH):
            for way in (0, 1):
                if reaches(way, d, k):
                    ring_copy(xall.at[t], t, d, k, way).wait_send()

    def cross_sent(h):
        for k in range(CH):
            cross_copy(xall.at[t], t, h, k).wait_send()

    def lr_sent():
        @pl.loop(1, NT)
        def _(i):
            lr_copy(i).wait_send()

    def expand():
        @pl.loop(1, NT)
        def _(i):
            src = lax.rem(t + NT - i, NT)
            pltpu.make_async_remote_copy(
                lr.at[src], lr.at[src], lr_send.at[i], lr_recv.at[i],
                device_id={"group": g, "tensor": tensor_peer(i)}, device_id_type=MESH).wait_recv()

        for r in range(RANK):
            lr2[r:r + 1, :] = lr[r]
        low = lr2[...].astype(jnp.bfloat16).astype(jnp.float32)
        idx = idx_ref[...]
        spread = jnp.concatenate([jnp.where(idx == s, low, 0.0) for s in range(SLOTS)], axis=0)
        spread = jnp.transpose(spread).astype(jnp.bfloat16)
        adapter = jnp.dot(spread, up_slots[...], preferred_element_type=jnp.float32)
        acc[...] += SCALE * adapter

    def operands_wait():
        x_copy.wait()
        w_copy.wait()

    ya_start(0)
    own_sends()
    ya_start(1)
    greet_groups()
    pick_adapters()
    operands_wait()
    panel_wait(0)
    groups_wait()
    send_adapters(0)
    ring_own(0)
    ring_step(1)
    panel_wait(1)
    send_adapters(1)
    ring_step(2, range(CH // 2))
    shrink()
    ring_step(2, range(CH // 2, CH))
    ring_own(1)
    ring_cross(0)
    ring_step(3, range(CH // 2))
    sum_shrink()
    ring_step(3, range(CH // 2, CH))
    ring_own(2)
    ring_cross(1)
    early_sends()
    ring_cross(2)
    ring_own(3)
    ring_sent(1)
    ring_sent(2)
    ring_sent(3)
    for h in (0, 1, 2, 6, 7):
        cross_sent(h)
    adapters_wait(1)
    ring_step(4)
    ring_cross(3)
    cross_sent(3)
    cross_sent(5)
    expand()
    lr_sent()
    ring_own(4)
    ring_cross(4)

    out_ref[...] = acc[...].astype(out_ref.dtype)
    ring_sent(NY // 2)
    cross_sent(NY // 2)


def body(tokens, token_slot_index, group_slot_adapters, adapter_storage_position, query_weight, down_weight, up_weight):
    hbm = pl.BlockSpec(memory_space=pltpu.HBM)
    vmem = pl.BlockSpec(memory_space=pltpu.VMEM)
    dma = pltpu.SemaphoreType.DMA
    bf16, f32 = jnp.bfloat16, jnp.float32
    return pl.pallas_call(
        kernel,
        out_shape=jax.ShapeDtypeStruct((ROWS, NB), bf16),
        in_specs=[hbm] * 7,
        out_specs=vmem,
        scratch_shapes=[
            pltpu.SMEM((SLOTS, NG), jnp.int32),
            pltpu.SMEM((NT * NG,), jnp.int32),
            pltpu.VMEM((1, ROWS), jnp.int32),
            pltpu.VMEM((NT, ROWS, KB), bf16),
            pltpu.VMEM((NT * KB, NB), bf16),
            pltpu.VMEM((NT, RANK, KB), bf16),
            pltpu.VMEM((NT, RANK, NB), bf16),
            pltpu.VMEM((NG, RANK, KB), bf16),
            pltpu.VMEM((NG, RANK, NB), bf16),
            pltpu.VMEM((NG, RANK, KB), bf16),
            pltpu.VMEM((NG, RANK, NB), bf16),
            pltpu.VMEM((SLOTS * RANK, KB), bf16),
            pltpu.VMEM((SLOTS * RANK, NB), bf16),
            pltpu.VMEM((ROWS, NB), f32),
            pltpu.VMEM((RANK, 1, ROWS), f32),
            pltpu.VMEM((NT, 1, ROWS), f32),
            pltpu.VMEM((NT, 1, ROWS), f32),
            pltpu.VMEM((RANK, ROWS), f32),
            pltpu.SMEM((NG,), jnp.int32),
            pltpu.SemaphoreType.REGULAR, pltpu.SemaphoreType.REGULAR,
            dma, dma, dma((2,)), dma((3,)),
            dma((2, NT)), dma((2, NT)), dma((2, NG)), dma((2, NG)),
            dma((2, NY // 2, CH)), dma((2, NY // 2, CH)), dma((NY, CH)), dma((NY, CH)),
            dma((NT,)), dma((NT,)), dma((NT,)), dma((NT,)),
        ],
        compiler_params=pltpu.CompilerParams(
            collective_id=0, has_side_effects=True, vmem_limit_bytes=VLIM * 1024),
        cost_estimate=pl.CostEstimate(flops=2 * ROWS * NT * KB * NB, bytes_accessed=8 << 20, transcendentals=0),
    )(group_slot_adapters.T, adapter_storage_position, token_slot_index.reshape(1, ROWS),
      tokens, query_weight, down_weight, up_weight)


def solution(mesh):
    in_specs = (
        P("group", "tensor"),
        P("group"),
        P(),
        P(),
        P(None, "tensor"),
        P(("group", "tensor"), None, None),
        P(("group", "tensor"), None, None),
    )
    return jax.shard_map(body, mesh=mesh, in_specs=in_specs, out_specs=P("group", "tensor"), check_vma=False)
```

```python
import functools

import jax
import jax.numpy as jnp
from jax import lax
from jax.experimental import pallas as pl
from jax.experimental.pallas import tpu as pltpu
from jax.sharding import PartitionSpec as P

RANK = 16
SLOTS = 16
SCALE = 0.5
NZ, NX, NY, NC = 8, 4, 8, 2
NG, NT = NZ * NX, NY * NC
ROWS = 512
KB = 512
NB = 256
CH = 4
CR = ROWS // CH
VLIM = 40 * 1024
PLUS = (0, 2)
MESH = pl.DeviceIdType.MESH


def kernel(
    gsa_hbm, asp_hbm, idx_hbm, tok, w_hbm, down, up, out_ref,
    gsa, asp, idx_ref, xall, w_v, down_panel, up_panel, down_staged, up_staged, down_inbox, up_inbox, down_slots, up_slots, acc, part, rs, lr, lr2, local_of, here, opened,
    w_sem, x_sem, own_sem, table_sem,
    ya_send, ya_recv, ga_send, ga_recv,
    ring_send, ring_recv, cross_send, cross_recv,
    rs_send, rs_recv, lr_send, lr_recv,
):
    g = lax.axis_index("group")
    t = lax.axis_index("tensor")
    y = t // NC
    c = t % NC
    other = y * NC + (1 - c)

    def tensor_peer(i):
        return lax.rem(t + i, NT)

    def group_peer(j):
        return lax.rem(g + j, NG)

    barrier = pltpu.get_barrier_semaphore()

    @pl.loop(1, NT)
    def _(i):
        dst = tensor_peer(i)

        @pl.when(dst != 0)
        def _():
            pl.semaphore_signal(barrier, inc=1, device_id={"group": g, "tensor": dst}, device_id_type=MESH)

    w_copy = pltpu.make_async_copy(w_hbm, w_v, w_sem)
    x_copy = pltpu.make_async_copy(tok, xall.at[t], x_sem)
    down_own = pltpu.make_async_copy(
        down.at[0, :, pl.ds(pl.multiple_of(t * KB, KB), KB)], down_panel.at[t], own_sem.at[0])
    up_own = pltpu.make_async_copy(
        up.at[0, :, pl.ds(pl.multiple_of(t * NB, NB), NB)], up_panel.at[t], own_sem.at[1])
    tables = [
        pltpu.make_async_copy(src, dst, table_sem.at[n])
        for n, (src, dst) in enumerate(((gsa_hbm, gsa), (asp_hbm, asp), (idx_hbm, idx_ref)))
    ]
    for copy in tables:
        copy.start()
    down_own.start()
    up_own.start()
    x_copy.start()
    w_copy.start()

    @pl.when(t != 0)
    def _():
        pl.semaphore_wait(barrier, NT - 1)

    @pl.when(t == 1)
    def _():
        pl.semaphore_signal(here, inc=1, device_id={"group": g, "tensor": t - 1}, device_id_type=MESH)

    @pl.when(t == 0)
    def _():
        pl.semaphore_wait(here, 1)

    def settled(block, send_sem, recv_sem):
        return pltpu.make_async_remote_copy(
            block, block, send_sem, recv_sem, device_id={"group": g, "tensor": other}, device_id_type=MESH)

    maps = (
        (down, KB, down_panel, down_staged, down_inbox, down_slots),
        (up, NB, up_panel, up_staged, up_inbox, up_slots),
    )

    def ya_copy(i, m):
        ref, width, panel = maps[m][:3]
        dst = tensor_peer(i)
        return pltpu.make_async_remote_copy(
            ref.at[0, :, pl.ds(pl.multiple_of(dst * width, width), width)], panel.at[t],
            ya_send.at[m], ya_recv.at[m], device_id={"group": g, "tensor": dst}, device_id_type=MESH)

    def ya_start(m):
        @pl.loop(1, NT)
        def _(i):
            ya_copy(i, m).start()

    def ya_all(m):
        return settled(maps[m][2].at[pl.ds(0, NT - 1)], ya_send.at[m], ya_recv.at[m])

    def ring_copy(src, block, d, k, way):
        dst_y = lax.rem(y + (1 if way == 0 else NY - 1), NY)
        rows = slice(k * CR, (k + 1) * CR)
        n = (d - 1) * 2 * CH + (2 * k + way if d < NY // 2 else k)
        return pltpu.make_async_remote_copy(
            src.at[rows, :], xall.at[block, rows, :], ring_send, ring_recv.at[n],
            device_id={"group": g, "tensor": dst_y * NC + c}, device_id_type=MESH)

    def cross_copy(src, block, h, k):
        rows = slice(k * CR, (k + 1) * CR)
        n = NY if h == NY // 2 and k >= CH // 2 else h
        return pltpu.make_async_remote_copy(
            src.at[rows, :], xall.at[block, rows, :], cross_send, cross_recv.at[n],
            device_id={"group": g, "tensor": other}, device_id_type=MESH)

    def cross_all(h):
        block = xall.at[0]
        if h in (NY // 2, NY):
            block = xall.at[0, pl.ds(0, ROWS // 2)]
        return settled(block, cross_send, cross_recv.at[h])

    def reaches(way, d, k):
        if d < NY // 2:
            return True
        return d == NY // 2 and (k in PLUS) == (way == 0)

    def source(way, d):
        ys = lax.rem(y + (NY - d if way == 0 else d), NY)
        return ys * NC + c, ys * NC + (1 - c)

    def own_sends():
        for k in range(CH):
            for way in (0, 1):
                ring_copy(tok, t, 1, k, way).start()
            cross_copy(tok, t, 0, k).start()

    def greet_groups():
        @pl.when(t == 0)
        def _():
            @pl.loop(1, NG)
            def _(j):
                pl.semaphore_signal(
                    barrier, inc=1, device_id={"group": group_peer(j), "tensor": t}, device_id_type=MESH)

    def pick_adapters():
        for copy in tables:
            copy.wait()

        @pl.loop(0, NG)
        def _(r):
            pick = jnp.int32(0)
            for s in range(SLOTS):
                place = asp[gsa[s, r]]
                pick = pick + jnp.where(lax.shift_right_logical(place, 4) == g, place & 15, 0)
            local_of[r] = pick

    def panel_wait(m):
        (down_own, up_own)[m].wait()

        ya_all(m).wait_recv()

    def groups_wait():
        @pl.when(t == 0)
        def _():
            pl.semaphore_wait(barrier, NG - 1)

            @pl.loop(1, NT)
            def _(i):
                pl.semaphore_signal(
                    opened, inc=1, device_id={"group": g, "tensor": tensor_peer(i)}, device_id_type=MESH)

        @pl.when(t != 0)
        def _():
            pl.semaphore_wait(opened, 1)

    def ga_copy(j, m):
        staged, inbox = maps[m][3:5]
        dst = group_peer(j)
        return pltpu.make_async_remote_copy(
            staged.at[j], inbox.at[g],
            ga_send.at[m], ga_recv.at[m], device_id={"group": dst, "tensor": t}, device_id_type=MESH)

    def send_adapters(m):
        panel, staged, inbox = maps[m][2:5]

        @pl.loop(1, NG)
        def _(j):
            staged[j] = panel[local_of[group_peer(j)]]
            ga_copy(j, m).start()

        inbox[g] = panel[local_of[g]]

    def ga_all(m):
        return settled(maps[m][4].at[pl.ds(0, NG - 1)], ga_send.at[m], ga_recv.at[m])

    def adapters_wait(m):
        inbox, slots = maps[m][4:]

        ga_all(m).wait_recv()

        for s in range(SLOTS):
            owner = lax.shift_right_logical(asp[gsa[s, g]], 4)
            slots[s * RANK:(s + 1) * RANK, :] = inbox[owner]

    def weight(block):
        return w_v[pl.ds(pl.multiple_of(block * KB, KB), KB), :]

    def accumulate(block, first=False):
        term = jnp.dot(xall[block], weight(block), preferred_element_type=jnp.float32)
        if first:
            acc[...] = term
        else:
            acc[...] += term

    def close(part_rows):
        far, far_other = source(0, NY // 2)
        rows = pl.ds(part_rows * (ROWS // 2), ROWS // 2)
        value = acc[rows, :] + jnp.dot(xall[far, rows, :], weight(far), preferred_element_type=jnp.float32)
        cross_all(NY if part_rows else NY // 2).wait_recv()
        value = value + jnp.dot(
            xall[far_other, rows, :], weight(far_other), preferred_element_type=jnp.float32)
        out_ref[rows, :] = value.astype(out_ref.dtype)

    def ring_step(d, ks=range(CH)):
        for k in ks:
            for way in (0, 1):
                if not reaches(way, d, k):
                    continue
                block, _ = source(way, d)
                ring_copy(xall.at[block], block, d, k, way).wait_recv()
                if reaches(way, d + 1, k):
                    ring_copy(xall.at[block], block, d + 1, k, way).start()
                h = d if way == 0 or d == NY // 2 else NY - d
                cross_copy(xall.at[block], block, h, k).start()

    def blocks_at(d):
        return (0,) if d == NY // 2 else (0, 1)

    def ring_own(d):
        if d == 0:
            accumulate(t, True)
            return
        for way in blocks_at(d):
            accumulate(source(way, d)[0])

    def ring_cross(d):
        for way in blocks_at(d) if d else (0,):
            h = d if way == 0 else NY - d
            block = source(way, d)[1]
            cross_all(h).wait_recv()
            accumulate(block)

    def rs_copy(i):
        dst = tensor_peer(i)
        return pltpu.make_async_remote_copy(
            part.at[dst], rs.at[t], rs_send, rs_recv,
            device_id={"group": g, "tensor": dst}, device_id_type=MESH)

    def rs_all():
        return settled(rs.at[pl.ds(0, NT - 1)], rs_send, rs_recv)

    def lr_all():
        return settled(lr.at[pl.ds(0, NT - 1)], lr_send, lr_recv)

    def lr_copy(i):
        return pltpu.make_async_remote_copy(
            lr.at[t], lr.at[t], lr_send, lr_recv,
            device_id={"group": g, "tensor": tensor_peer(i)}, device_id_type=MESH)

    def shrink():
        adapters_wait(0)
        idx = idx_ref[...]
        every = lax.dot_general(
            down_slots[...], xall[t], (((1,), (1,)), ((), ())), preferred_element_type=jnp.float32)
        partial = jnp.zeros((RANK, ROWS), jnp.float32)
        for s in range(SLOTS):
            partial = partial + jnp.where(idx == s, every[s * RANK:(s + 1) * RANK, :], 0.0)
        for r in range(RANK):
            part[r] = partial[r:r + 1, :]

        @pl.loop(1, NT)
        def _(i):
            rs_copy(i).start()

        rs[t] = part[t]

    def sum_shrink():
        rs_all().wait_recv()

        total = rs[0]
        for i in range(1, NT):
            total = total + rs[i]
        lr[t] = total

        @pl.loop(1, NT)
        def _(i):
            lr_copy(i).start()

    def early_sends():
        for m in (0, 1):
            ya_all(m).wait_send()
            ga_all(m).wait_send()
        rs_all().wait_send()

    def last_sends():
        lr_all().wait_send()
        settled(xall.at[pl.ds(0, NY - 1)], ring_send, ring_recv.at[0]).wait_send()
        settled(xall.at[pl.ds(0, NY)], cross_send, cross_recv.at[0]).wait_send()

    def expand():
        lr_all().wait_recv()

        for r in range(RANK):
            lr2[r:r + 1, :] = lr[r]
        low = lr2[...].astype(jnp.bfloat16).astype(jnp.float32)
        idx = idx_ref[...]
        spread = jnp.concatenate([jnp.where(idx == s, low, 0.0) for s in range(SLOTS)], axis=0)
        spread = jnp.transpose(spread).astype(jnp.bfloat16)
        adapter = jnp.dot(spread, up_slots[...], preferred_element_type=jnp.float32)
        acc[...] += SCALE * adapter

    def operands_wait():
        x_copy.wait()
        w_copy.wait()

    ya_start(0)
    own_sends()
    ya_start(1)
    greet_groups()
    pick_adapters()
    operands_wait()
    panel_wait(0)
    groups_wait()
    send_adapters(0)
    ring_own(0)
    ring_step(1)
    panel_wait(1)
    send_adapters(1)
    ring_step(2, range(CH // 2))
    shrink()
    ring_step(2, range(CH // 2, CH))
    ring_own(1)
    ring_cross(0)
    ring_step(3, range(CH // 2))
    sum_shrink()
    ring_step(3, range(CH // 2, CH))
    ring_own(2)
    ring_cross(1)
    early_sends()
    ring_cross(2)
    ring_own(3)
    adapters_wait(1)
    ring_step(4, range(CH // 2))
    ring_cross(3)
    expand()
    close(0)
    ring_step(4, range(CH // 2, CH))
    close(1)

    last_sends()


def body(tokens, token_slot_index, group_slot_adapters, adapter_storage_position, query_weight, down_weight, up_weight):
    hbm = pl.BlockSpec(memory_space=pltpu.HBM)
    vmem = pl.BlockSpec(memory_space=pltpu.VMEM)
    dma = pltpu.SemaphoreType.DMA
    bf16, f32 = jnp.bfloat16, jnp.float32
    return pl.pallas_call(
        kernel,
        out_shape=jax.ShapeDtypeStruct((ROWS, NB), bf16),
        in_specs=[hbm] * 7,
        out_specs=vmem,
        scratch_shapes=[
            pltpu.SMEM((SLOTS, NG), jnp.int32),
            pltpu.SMEM((NT * NG,), jnp.int32),
            pltpu.VMEM((1, ROWS), jnp.int32),
            pltpu.VMEM((NT, ROWS, KB), bf16),
            pltpu.VMEM((NT * KB, NB), bf16),
            pltpu.VMEM((NT, RANK, KB), bf16),
            pltpu.VMEM((NT, RANK, NB), bf16),
            pltpu.VMEM((NG, RANK, KB), bf16),
            pltpu.VMEM((NG, RANK, NB), bf16),
            pltpu.VMEM((NG, RANK, KB), bf16),
            pltpu.VMEM((NG, RANK, NB), bf16),
            pltpu.VMEM((SLOTS * RANK, KB), bf16),
            pltpu.VMEM((SLOTS * RANK, NB), bf16),
            pltpu.VMEM((ROWS, NB), f32),
            pltpu.VMEM((RANK, 1, ROWS), f32),
            pltpu.VMEM((NT, 1, ROWS), f32),
            pltpu.VMEM((NT, 1, ROWS), f32),
            pltpu.VMEM((RANK, ROWS), f32),
            pltpu.SMEM((NG,), jnp.int32),
            pltpu.SemaphoreType.REGULAR, pltpu.SemaphoreType.REGULAR,
            dma, dma, dma((2,)), dma((3,)),
            dma((2,)), dma((2,)), dma((2,)), dma((2,)),
            dma, dma(((NY - 1) * CH,)), dma, dma((NY + 1,)),
            dma, dma, dma, dma,
        ],
        compiler_params=pltpu.CompilerParams(
            collective_id=0, has_side_effects=True, vmem_limit_bytes=VLIM * 1024),
        cost_estimate=pl.CostEstimate(flops=2 * ROWS * NT * KB * NB, bytes_accessed=8 << 20, transcendentals=0),
    )(*(pltpu.with_memory_space_constraint(x, pltpu.HBM) for x in (
        group_slot_adapters.T, adapter_storage_position, token_slot_index.reshape(1, ROWS),
        tokens, query_weight, down_weight, up_weight)))


def solution(mesh):
    in_specs = (
        P("group", "tensor"),
        P("group"),
        P(),
        P(),
        P(None, "tensor"),
        P(("group", "tensor"), None, None),
        P(("group", "tensor"), None, None),
    )
    return jax.shard_map(body, mesh=mesh, in_specs=in_specs, out_specs=P("group", "tensor"), check_vma=False)
```

```python
import functools

import jax
import jax.numpy as jnp
from jax import lax
from jax.experimental import pallas as pl
from jax.experimental.pallas import tpu as pltpu
from jax.sharding import PartitionSpec as P

RANK = 16
SLOTS = 16
SCALE = 0.5
NZ, NX, NY, NC = 8, 4, 8, 2
NG, NT = NZ * NX, NY * NC
ROWS = 512
KB = 512
NB = 256
CH = 4
CR = ROWS // CH
VLIM = 40 * 1024
PLUS = (0, 2)
MESH = pl.DeviceIdType.MESH


def kernel(
    gsa_hbm, asp_hbm, idx_hbm, tok, w_hbm, down, up, out_ref,
    gsa, asp, idx_ref, xall, w_v, down_panel, up_panel, down_staged, up_staged, down_inbox, up_inbox, down_slots, up_slots, acc, part, rs, lr, lr2, local_of, here, opened,
    w_sem, x_sem, own_sem, table_sem,
    ya_send, ya_recv, ga_send, ga_recv,
    ring_send, ring_recv, cross_send, cross_recv,
    rs_send, rs_recv, lr_send, lr_recv,
):
    g = lax.axis_index("group")
    t = lax.axis_index("tensor")
    y = t // NC
    c = t % NC
    other = y * NC + (1 - c)

    def tensor_peer(i):
        return lax.rem(t + NT + (2 * lax.rem(i, 2) - 1) * lax.div(i + 1, 2), NT)

    def group_peer(j):
        return lax.rem(g + NG + (2 * lax.rem(j, 2) - 1) * lax.div(j + 1, 2), NG)

    barrier = pltpu.get_barrier_semaphore()

    @pl.loop(1, NT)
    def _(i):
        dst = tensor_peer(i)

        @pl.when(dst != 0)
        def _():
            pl.semaphore_signal(barrier, inc=1, device_id={"group": g, "tensor": dst}, device_id_type=MESH)

    w_copy = pltpu.make_async_copy(w_hbm, w_v, w_sem)
    x_copy = pltpu.make_async_copy(tok, xall.at[t], x_sem)
    down_own = pltpu.make_async_copy(
        down.at[0, :, pl.ds(pl.multiple_of(t * KB, KB), KB)], down_panel.at[t], own_sem.at[0])
    up_own = pltpu.make_async_copy(
        up.at[0, :, pl.ds(pl.multiple_of(t * NB, NB), NB)], up_panel.at[t], own_sem.at[1])
    tables = [
        pltpu.make_async_copy(src, dst, table_sem.at[n])
        for n, (src, dst) in enumerate(((gsa_hbm, gsa), (asp_hbm, asp), (idx_hbm, idx_ref)))
    ]
    for copy in tables:
        copy.start()
    down_own.start()
    up_own.start()
    x_copy.start()
    w_copy.start()

    @pl.when(t != 0)
    def _():
        pl.semaphore_wait(barrier, NT - 1)

    @pl.when(t == 1)
    def _():
        pl.semaphore_signal(here, inc=1, device_id={"group": g, "tensor": t - 1}, device_id_type=MESH)

    @pl.when(t == 0)
    def _():
        pl.semaphore_wait(here, 1)

    def settled(block, send_sem, recv_sem):
        return pltpu.make_async_remote_copy(
            block, block, send_sem, recv_sem, device_id={"group": g, "tensor": other}, device_id_type=MESH)

    maps = (
        (down, KB, down_panel, down_staged, down_inbox, down_slots),
        (up, NB, up_panel, up_staged, up_inbox, up_slots),
    )

    def ya_copy(i, m):
        ref, width, panel = maps[m][:3]
        dst = tensor_peer(i)
        return pltpu.make_async_remote_copy(
            ref.at[0, :, pl.ds(pl.multiple_of(dst * width, width), width)], panel.at[t],
            ya_send.at[m], ya_recv.at[m], device_id={"group": g, "tensor": dst}, device_id_type=MESH)

    def ya_start(m):
        @pl.loop(1, NT)
        def _(i):
            ya_copy(i, m).start()

    def ya_all(m):
        return settled(maps[m][2].at[pl.ds(0, NT - 1)], ya_send.at[m], ya_recv.at[m])

    def ring_copy(src, block, d, k, way):
        dst_y = lax.rem(y + (1 if way == 0 else NY - 1), NY)
        rows = slice(k * CR, (k + 1) * CR)
        n = (d - 1) * 2 * CH + (2 * k + way if d < NY // 2 else k)
        return pltpu.make_async_remote_copy(
            src.at[rows, :], xall.at[block, rows, :], ring_send, ring_recv.at[n],
            device_id={"group": g, "tensor": dst_y * NC + c}, device_id_type=MESH)

    def cross_copy(src, block, h, k):
        rows = slice(k * CR, (k + 1) * CR)
        n = NY if h == NY // 2 and k >= CH // 2 else h
        return pltpu.make_async_remote_copy(
            src.at[rows, :], xall.at[block, rows, :], cross_send, cross_recv.at[n],
            device_id={"group": g, "tensor": other}, device_id_type=MESH)

    def cross_all(h):
        block = xall.at[0]
        if h in (NY // 2, NY):
            block = xall.at[0, pl.ds(0, ROWS // 2)]
        return settled(block, cross_send, cross_recv.at[h])

    def reaches(way, d, k):
        if d < NY // 2:
            return True
        return d == NY // 2 and (k in PLUS) == (way == 0)

    def source(way, d):
        ys = lax.rem(y + (NY - d if way == 0 else d), NY)
        return ys * NC + c, ys * NC + (1 - c)

    def own_sends():
        for k in range(CH):
            for way in (0, 1):
                ring_copy(tok, t, 1, k, way).start()
            cross_copy(tok, t, 0, k).start()

    def greet_groups():
        @pl.when(t == 0)
        def _():
            @pl.loop(1, NG)
            def _(j):
                pl.semaphore_signal(
                    barrier, inc=1, device_id={"group": group_peer(j), "tensor": t}, device_id_type=MESH)

    def pick_adapters():
        for copy in tables:
            copy.wait()

        @pl.loop(0, NG)
        def _(r):
            pick = jnp.int32(0)
            for s in range(SLOTS):
                place = asp[gsa[s, r]]
                pick = pick + jnp.where(lax.shift_right_logical(place, 4) == g, place & 15, 0)
            local_of[r] = pick

    def panel_wait(m):
        (down_own, up_own)[m].wait()

        ya_all(m).wait_recv()

    def groups_wait():
        @pl.when(t == 0)
        def _():
            pl.semaphore_wait(barrier, NG - 1)

            @pl.loop(1, NT)
            def _(i):
                pl.semaphore_signal(
                    opened, inc=1, device_id={"group": g, "tensor": tensor_peer(i)}, device_id_type=MESH)

        @pl.when(t != 0)
        def _():
            pl.semaphore_wait(opened, 1)

    def ga_copy(j, m):
        staged, inbox = maps[m][3:5]
        dst = group_peer(j)
        return pltpu.make_async_remote_copy(
            staged.at[j], inbox.at[g],
            ga_send.at[m], ga_recv.at[m], device_id={"group": dst, "tensor": t}, device_id_type=MESH)

    def send_adapters(m):
        panel, staged, inbox = maps[m][2:5]

        @pl.loop(1, NG)
        def _(j):
            staged[j] = panel[local_of[group_peer(j)]]
            ga_copy(j, m).start()

        inbox[g] = panel[local_of[g]]

    def ga_all(m):
        return settled(maps[m][4].at[pl.ds(0, NG - 1)], ga_send.at[m], ga_recv.at[m])

    def adapters_wait(m):
        inbox, slots = maps[m][4:]

        ga_all(m).wait_recv()

        for s in range(SLOTS):
            owner = lax.shift_right_logical(asp[gsa[s, g]], 4)
            slots[s * RANK:(s + 1) * RANK, :] = inbox[owner]

    def weight(block):
        return w_v[pl.ds(pl.multiple_of(block * KB, KB), KB), :]

    def accumulate(block, first=False):
        term = jnp.dot(xall[block], weight(block), preferred_element_type=jnp.float32)
        if first:
            acc[...] = term
        else:
            acc[...] += term

    def close(part_rows):
        far, far_other = source(0, NY // 2)
        rows = pl.ds(part_rows * (ROWS // 2), ROWS // 2)
        value = acc[rows, :] + jnp.dot(xall[far, rows, :], weight(far), preferred_element_type=jnp.float32)
        cross_all(NY if part_rows else NY // 2).wait_recv()
        value = value + jnp.dot(
            xall[far_other, rows, :], weight(far_other), preferred_element_type=jnp.float32)
        out_ref[rows, :] = value.astype(out_ref.dtype)

    def ring_step(d, ks=range(CH)):
        for k in ks:
            for way in (0, 1):
                if not reaches(way, d, k):
                    continue
                block, _ = source(way, d)
                ring_copy(xall.at[block], block, d, k, way).wait_recv()
                if reaches(way, d + 1, k):
                    ring_copy(xall.at[block], block, d + 1, k, way).start()
                h = d if way == 0 or d == NY // 2 else NY - d
                cross_copy(xall.at[block], block, h, k).start()

    def blocks_at(d):
        return (0,) if d == NY // 2 else (0, 1)

    def ring_own(d):
        if d == 0:
            accumulate(t, True)
            return
        for way in blocks_at(d):
            accumulate(source(way, d)[0])

    def ring_cross(d):
        for way in blocks_at(d) if d else (0,):
            h = d if way == 0 else NY - d
            block = source(way, d)[1]
            cross_all(h).wait_recv()
            accumulate(block)

    def rs_copy(i):
        dst = tensor_peer(i)
        return pltpu.make_async_remote_copy(
            part.at[dst], rs.at[t], rs_send, rs_recv,
            device_id={"group": g, "tensor": dst}, device_id_type=MESH)

    def rs_all():
        return settled(rs.at[pl.ds(0, NT - 1)], rs_send, rs_recv)

    def lr_all():
        return settled(lr.at[pl.ds(0, NT - 1)], lr_send, lr_recv)

    def lr_copy(i):
        return pltpu.make_async_remote_copy(
            lr.at[t], lr.at[t], lr_send, lr_recv,
            device_id={"group": g, "tensor": tensor_peer(i)}, device_id_type=MESH)

    def shrink():
        adapters_wait(0)
        idx = idx_ref[...]
        every = lax.dot_general(
            down_slots[...], xall[t], (((1,), (1,)), ((), ())), preferred_element_type=jnp.float32)
        partial = jnp.zeros((RANK, ROWS), jnp.float32)
        for s in range(SLOTS):
            partial = partial + jnp.where(idx == s, every[s * RANK:(s + 1) * RANK, :], 0.0)
        for r in range(RANK):
            part[r] = partial[r:r + 1, :]

        @pl.loop(1, NT)
        def _(i):
            rs_copy(i).start()

        rs[t] = part[t]

    def sum_shrink():
        rs_all().wait_recv()

        total = rs[0]
        for i in range(1, NT):
            total = total + rs[i]
        lr[t] = total

        @pl.loop(1, NT)
        def _(i):
            lr_copy(i).start()

    def early_sends():
        for m in (0, 1):
            ya_all(m).wait_send()
            ga_all(m).wait_send()
        rs_all().wait_send()

    def last_sends():
        lr_all().wait_send()
        settled(xall.at[pl.ds(0, NY - 1)], ring_send, ring_recv.at[0]).wait_send()
        settled(xall.at[pl.ds(0, NY)], cross_send, cross_recv.at[0]).wait_send()

    def expand():
        lr_all().wait_recv()

        for r in range(RANK):
            lr2[r:r + 1, :] = lr[r]
        low = lr2[...].astype(jnp.bfloat16).astype(jnp.float32)
        idx = idx_ref[...]
        spread = jnp.concatenate([jnp.where(idx == s, low, 0.0) for s in range(SLOTS)], axis=0)
        spread = jnp.transpose(spread).astype(jnp.bfloat16)
        adapter = jnp.dot(spread, up_slots[...], preferred_element_type=jnp.float32)
        acc[...] += SCALE * adapter

    def operands_wait():
        x_copy.wait()
        w_copy.wait()

    ya_start(0)
    own_sends()
    ya_start(1)
    greet_groups()
    pick_adapters()
    operands_wait()
    panel_wait(0)
    groups_wait()
    send_adapters(0)
    ring_own(0)
    ring_step(1)
    panel_wait(1)
    send_adapters(1)
    shrink()
    ring_step(2)
    ring_own(1)
    ring_cross(0)
    sum_shrink()
    ring_step(3)
    ring_own(2)
    ring_cross(1)
    early_sends()
    ring_cross(2)
    ring_own(3)
    adapters_wait(1)
    ring_step(4, range(CH // 2))
    ring_cross(3)
    expand()
    close(0)
    ring_step(4, range(CH // 2, CH))
    close(1)
    last_sends()


def body(tokens, token_slot_index, group_slot_adapters, adapter_storage_position, query_weight, down_weight, up_weight):
    hbm = pl.BlockSpec(memory_space=pltpu.HBM)
    vmem = pl.BlockSpec(memory_space=pltpu.VMEM)
    dma = pltpu.SemaphoreType.DMA
    bf16, f32 = jnp.bfloat16, jnp.float32
    return pl.pallas_call(
        kernel,
        out_shape=jax.ShapeDtypeStruct((ROWS, NB), bf16),
        in_specs=[hbm] * 7,
        out_specs=vmem,
        scratch_shapes=[
            pltpu.SMEM((SLOTS, NG), jnp.int32),
            pltpu.SMEM((NT * NG,), jnp.int32),
            pltpu.VMEM((1, ROWS), jnp.int32),
            pltpu.VMEM((NT, ROWS, KB), bf16),
            pltpu.VMEM((NT * KB, NB), bf16),
            pltpu.VMEM((NT, RANK, KB), bf16),
            pltpu.VMEM((NT, RANK, NB), bf16),
            pltpu.VMEM((NG, RANK, KB), bf16),
            pltpu.VMEM((NG, RANK, NB), bf16),
            pltpu.VMEM((NG, RANK, KB), bf16),
            pltpu.VMEM((NG, RANK, NB), bf16),
            pltpu.VMEM((SLOTS * RANK, KB), bf16),
            pltpu.VMEM((SLOTS * RANK, NB), bf16),
            pltpu.VMEM((ROWS, NB), f32),
            pltpu.VMEM((RANK, 1, ROWS), f32),
            pltpu.VMEM((NT, 1, ROWS), f32),
            pltpu.VMEM((NT, 1, ROWS), f32),
            pltpu.VMEM((RANK, ROWS), f32),
            pltpu.SMEM((NG,), jnp.int32),
            pltpu.SemaphoreType.REGULAR, pltpu.SemaphoreType.REGULAR,
            dma, dma, dma((2,)), dma((3,)),
            dma((2,)), dma((2,)), dma((2,)), dma((2,)),
            dma, dma(((NY - 1) * CH,)), dma, dma((NY + 1,)),
            dma, dma, dma, dma,
        ],
        compiler_params=pltpu.CompilerParams(
            collective_id=0, has_side_effects=True, vmem_limit_bytes=VLIM * 1024),
        cost_estimate=pl.CostEstimate(flops=2 * ROWS * NT * KB * NB, bytes_accessed=8 << 20, transcendentals=0),
    )(*(pltpu.with_memory_space_constraint(x, pltpu.HBM) for x in (
        group_slot_adapters.T, adapter_storage_position, token_slot_index.reshape(1, ROWS),
        tokens, query_weight, down_weight, up_weight)))


def solution(mesh):
    in_specs = (
        P("group", "tensor"),
        P("group"),
        P(),
        P(),
        P(None, "tensor"),
        P(("group", "tensor"), None, None),
        P(("group", "tensor"), None, None),
    )
    return jax.shard_map(body, mesh=mesh, in_specs=in_specs, out_specs=P("group", "tensor"), check_vma=False)
```

```python
import functools

import jax
import jax.numpy as jnp
from jax import lax
from jax.experimental import pallas as pl
from jax.experimental.pallas import tpu as pltpu
from jax.sharding import PartitionSpec as P

RANK = 16
SLOTS = 16
SCALE = 0.5
NZ, NX, NY, NC = 8, 4, 8, 2
NG, NT = NZ * NX, NY * NC
ROWS = 512
KB = 512
NB = 256
CH = 4
CR = ROWS // CH
VLIM = 40 * 1024
PLUS = (0, 2)
MESH = pl.DeviceIdType.MESH


def kernel(
    gsa_hbm, asp_hbm, idx_hbm, tok, w_hbm, down, up, out_ref,
    gsa, asp, idx_ref, xall, w_v, down_panel, up_panel, down_staged, up_staged, down_inbox, up_inbox, down_slots, up_slots, acc, part, rs, lr, lr2, local_of, here, opened,
    w_sem, x_sem, own_sem, table_sem,
    ya_send, ya_recv, ga_send, ga_recv,
    ring_send, ring_recv, cross_send, cross_recv,
    rs_send, rs_recv, lr_send, lr_recv,
):
    g = lax.axis_index("group")
    t = lax.axis_index("tensor")
    y = t // NC
    c = t % NC
    other = y * NC + (1 - c)

    def tensor_peer(i):
        return lax.rem(t + NT + (2 * lax.rem(i, 2) - 1) * lax.div(i + 1, 2), NT)

    def group_peer(j):
        return lax.rem(g + NG + (2 * lax.rem(j, 2) - 1) * lax.div(j + 1, 2), NG)

    barrier = pltpu.get_barrier_semaphore()

    @pl.loop(1, NT)
    def _(i):
        dst = tensor_peer(i)

        @pl.when(dst != 0)
        def _():
            pl.semaphore_signal(barrier, inc=1, device_id={"group": g, "tensor": dst}, device_id_type=MESH)

    w_copy = pltpu.make_async_copy(w_hbm, w_v, w_sem)
    x_copy = pltpu.make_async_copy(tok, xall.at[t], x_sem)
    down_own = pltpu.make_async_copy(
        down.at[0, :, pl.ds(pl.multiple_of(t * KB, KB), KB)], down_panel.at[t], own_sem.at[0])
    up_own = pltpu.make_async_copy(
        up.at[0, :, pl.ds(pl.multiple_of(t * NB, NB), NB)], up_panel.at[t], own_sem.at[1])
    tables = [
        pltpu.make_async_copy(src, dst, table_sem.at[n])
        for n, (src, dst) in enumerate(((gsa_hbm, gsa), (asp_hbm, asp), (idx_hbm, idx_ref)))
    ]
    for copy in tables:
        copy.start()
    down_own.start()
    up_own.start()
    x_copy.start()
    w_copy.start()

    @pl.when(t != 0)
    def _():
        pl.semaphore_wait(barrier, NT - 1)

    @pl.when(t == 1)
    def _():
        pl.semaphore_signal(here, inc=1, device_id={"group": g, "tensor": t - 1}, device_id_type=MESH)

    @pl.when(t == 0)
    def _():
        pl.semaphore_wait(here, 1)

    def settled(block, send_sem, recv_sem):
        return pltpu.make_async_remote_copy(
            block, block, send_sem, recv_sem, device_id={"group": g, "tensor": other}, device_id_type=MESH)

    maps = (
        (down, KB, down_panel, down_staged, down_inbox, down_slots),
        (up, NB, up_panel, up_staged, up_inbox, up_slots),
    )

    def ya_copy(i, m):
        ref, width, panel = maps[m][:3]
        dst = tensor_peer(i)
        return pltpu.make_async_remote_copy(
            ref.at[0, :, pl.ds(pl.multiple_of(dst * width, width), width)], panel.at[t],
            ya_send.at[m], ya_recv.at[m], device_id={"group": g, "tensor": dst}, device_id_type=MESH)

    def ya_start(m):
        @pl.loop(1, NT)
        def _(i):
            ya_copy(i, m).start()

    def ya_all(m):
        return settled(maps[m][2].at[pl.ds(0, NT - 1)], ya_send.at[m], ya_recv.at[m])

    def ring_copy(src, block, d, k, way):
        dst_y = lax.rem(y + (1 if way == 0 else NY - 1), NY)
        rows = slice(k * CR, (k + 1) * CR)
        n = (d - 1) * 2 * CH + (2 * k + way if d < NY // 2 else k)
        return pltpu.make_async_remote_copy(
            src.at[rows, :], xall.at[block, rows, :], ring_send, ring_recv.at[n],
            device_id={"group": g, "tensor": dst_y * NC + c}, device_id_type=MESH)

    def cross_copy(src, block, h, k):
        rows = slice(k * CR, (k + 1) * CR)
        n = NY if h == NY // 2 and k >= CH // 2 else h
        return pltpu.make_async_remote_copy(
            src.at[rows, :], xall.at[block, rows, :], cross_send, cross_recv.at[n],
            device_id={"group": g, "tensor": other}, device_id_type=MESH)

    def cross_all(h):
        block = xall.at[0]
        if h in (NY // 2, NY):
            block = xall.at[0, pl.ds(0, ROWS // 2)]
        return settled(block, cross_send, cross_recv.at[h])

    def reaches(way, d, k):
        if d < NY // 2:
            return True
        return d == NY // 2 and (k in PLUS) == (way == 0)

    def source(way, d):
        ys = lax.rem(y + (NY - d if way == 0 else d), NY)
        return ys * NC + c, ys * NC + (1 - c)

    def own_sends():
        for k in range(CH):
            for way in (0, 1):
                ring_copy(tok, t, 1, k, way).start()
            cross_copy(tok, t, 0, k).start()

    def greet_groups():
        @pl.when(t == 0)
        def _():
            @pl.loop(1, NG)
            def _(j):
                pl.semaphore_signal(
                    barrier, inc=1, device_id={"group": group_peer(j), "tensor": t}, device_id_type=MESH)

    def pick_adapters():
        for copy in tables:
            copy.wait()

        @pl.loop(0, NG)
        def _(r):
            pick = jnp.int32(0)
            for s in range(SLOTS):
                place = asp[gsa[s, r]]
                pick = pick + jnp.where(lax.shift_right_logical(place, 4) == g, place & 15, 0)
            local_of[r] = pick

    def panel_wait(m):
        (down_own, up_own)[m].wait()

        ya_all(m).wait_recv()

    def groups_wait():
        @pl.when(t == 0)
        def _():
            pl.semaphore_wait(barrier, NG - 1)

            @pl.loop(1, NT)
            def _(i):
                pl.semaphore_signal(
                    opened, inc=1, device_id={"group": g, "tensor": tensor_peer(i)}, device_id_type=MESH)

        @pl.when(t != 0)
        def _():
            pl.semaphore_wait(opened, 1)

    def ga_copy(j, m):
        staged, inbox = maps[m][3:5]
        dst = group_peer(j)
        return pltpu.make_async_remote_copy(
            staged.at[j], inbox.at[g],
            ga_send.at[m], ga_recv.at[m], device_id={"group": dst, "tensor": t}, device_id_type=MESH)

    def send_adapters(m):
        panel, staged, inbox = maps[m][2:5]

        @pl.loop(1, NG)
        def _(j):
            staged[j] = panel[local_of[group_peer(j)]]
            ga_copy(j, m).start()

        inbox[g] = panel[local_of[g]]

    def ga_all(m):
        return settled(maps[m][4].at[pl.ds(0, NG - 1)], ga_send.at[m], ga_recv.at[m])

    def adapters_wait(m):
        inbox, slots = maps[m][4:]

        ga_all(m).wait_recv()

        for s in range(SLOTS):
            owner = lax.shift_right_logical(asp[gsa[s, g]], 4)
            slots[s * RANK:(s + 1) * RANK, :] = inbox[owner]

    def weight(block):
        return w_v[pl.ds(pl.multiple_of(block * KB, KB), KB), :]

    def accumulate(block, first=False):
        term = jnp.dot(xall[block], weight(block), preferred_element_type=jnp.float32)
        if first:
            acc[...] = term
        else:
            acc[...] += term

    def close(part_rows):
        far, far_other = source(0, NY // 2)
        rows = pl.ds(part_rows * (ROWS // 2), ROWS // 2)
        value = acc[rows, :] + jnp.dot(xall[far, rows, :], weight(far), preferred_element_type=jnp.float32)
        cross_all(NY if part_rows else NY // 2).wait_recv()
        value = value + jnp.dot(
            xall[far_other, rows, :], weight(far_other), preferred_element_type=jnp.float32)
        out_ref[rows, :] = value.astype(out_ref.dtype)

    def ring_step(d, ks=range(CH)):
        for k in ks:
            for way in (0, 1):
                if not reaches(way, d, k):
                    continue
                block, _ = source(way, d)
                ring_copy(xall.at[block], block, d, k, way).wait_recv()
                if reaches(way, d + 1, k):
                    ring_copy(xall.at[block], block, d + 1, k, way).start()
                h = d if way == 0 or d == NY // 2 else NY - d
                cross_copy(xall.at[block], block, h, k).start()

    def blocks_at(d):
        return (0,) if d == NY // 2 else (0, 1)

    def ring_own(d):
        if d == 0:
            accumulate(t, True)
            return
        for way in blocks_at(d):
            accumulate(source(way, d)[0])

    def ring_cross(d):
        for way in blocks_at(d) if d else (0,):
            h = d if way == 0 else NY - d
            block = source(way, d)[1]
            cross_all(h).wait_recv()
            accumulate(block)

    def rs_copy(i):
        dst = tensor_peer(i)
        return pltpu.make_async_remote_copy(
            part.at[dst], rs.at[t], rs_send, rs_recv,
            device_id={"group": g, "tensor": dst}, device_id_type=MESH)

    def rs_all():
        return settled(rs.at[pl.ds(0, NT - 1)], rs_send, rs_recv)

    def lr_all():
        return settled(lr.at[pl.ds(0, NT - 1)], lr_send, lr_recv)

    def lr_copy(i):
        return pltpu.make_async_remote_copy(
            lr.at[t], lr.at[t], lr_send, lr_recv,
            device_id={"group": g, "tensor": tensor_peer(i)}, device_id_type=MESH)

    def shrink():
        adapters_wait(0)
        idx = idx_ref[...]
        every = lax.dot_general(
            down_slots[...], xall[t], (((1,), (1,)), ((), ())), preferred_element_type=jnp.float32)
        partial = jnp.zeros((RANK, ROWS), jnp.float32)
        for s in range(SLOTS):
            partial = partial + jnp.where(idx == s, every[s * RANK:(s + 1) * RANK, :], 0.0)
        for r in range(RANK):
            part[r] = partial[r:r + 1, :]

        @pl.loop(1, NT)
        def _(i):
            rs_copy(i).start()

        rs[t] = part[t]

    def sum_shrink():
        rs_all().wait_recv()

        total = rs[0]
        for i in range(1, NT):
            total = total + rs[i]
        lr[t] = total

        @pl.loop(1, NT)
        def _(i):
            lr_copy(i).start()

    def early_sends():
        for m in (0, 1):
            ya_all(m).wait_send()
            ga_all(m).wait_send()
        rs_all().wait_send()

    def last_sends():
        lr_all().wait_send()
        settled(xall.at[pl.ds(0, NY - 1)], ring_send, ring_recv.at[0]).wait_send()
        settled(xall.at[pl.ds(0, NY)], cross_send, cross_recv.at[0]).wait_send()

    def expand():
        lr_all().wait_recv()

        for r in range(RANK):
            lr2[r:r + 1, :] = lr[r]
        low = lr2[...].astype(jnp.bfloat16).astype(jnp.float32)
        idx = idx_ref[...]
        spread = jnp.concatenate([jnp.where(idx == s, low, 0.0) for s in range(SLOTS)], axis=0)
        spread = jnp.transpose(spread).astype(jnp.bfloat16)
        adapter = jnp.dot(spread, up_slots[...], preferred_element_type=jnp.float32)
        acc[...] += SCALE * adapter

    def operands_wait():
        x_copy.wait()
        w_copy.wait()

    ya_start(0)
    own_sends()
    ya_start(1)
    greet_groups()
    pick_adapters()
    operands_wait()
    panel_wait(0)
    groups_wait()
    send_adapters(0)
    ring_own(0)
    ring_step(1)
    panel_wait(1)
    send_adapters(1)
    shrink()
    ring_step(2)
    ring_own(1)
    ring_cross(0)
    sum_shrink()
    ring_step(3)
    ring_own(2)
    ring_cross(1)
    early_sends()
    ring_cross(2)
    ring_own(3)
    ring_step(4, range(CH // 2))
    ring_cross(3)
    ring_step(4, range(CH // 2, CH))
    adapters_wait(1)
    expand()
    close(0)
    close(1)
    last_sends()


def body(tokens, token_slot_index, group_slot_adapters, adapter_storage_position, query_weight, down_weight, up_weight):
    hbm = pl.BlockSpec(memory_space=pltpu.HBM)
    vmem = pl.BlockSpec(memory_space=pltpu.VMEM)
    dma = pltpu.SemaphoreType.DMA
    bf16, f32 = jnp.bfloat16, jnp.float32
    return pl.pallas_call(
        kernel,
        out_shape=jax.ShapeDtypeStruct((ROWS, NB), bf16),
        in_specs=[hbm] * 7,
        out_specs=vmem,
        scratch_shapes=[
            pltpu.SMEM((SLOTS, NG), jnp.int32),
            pltpu.SMEM((NT * NG,), jnp.int32),
            pltpu.VMEM((1, ROWS), jnp.int32),
            pltpu.VMEM((NT, ROWS, KB), bf16),
            pltpu.VMEM((NT * KB, NB), bf16),
            pltpu.VMEM((NT, RANK, KB), bf16),
            pltpu.VMEM((NT, RANK, NB), bf16),
            pltpu.VMEM((NG, RANK, KB), bf16),
            pltpu.VMEM((NG, RANK, NB), bf16),
            pltpu.VMEM((NG, RANK, KB), bf16),
            pltpu.VMEM((NG, RANK, NB), bf16),
            pltpu.VMEM((SLOTS * RANK, KB), bf16),
            pltpu.VMEM((SLOTS * RANK, NB), bf16),
            pltpu.VMEM((ROWS, NB), f32),
            pltpu.VMEM((RANK, 1, ROWS), f32),
            pltpu.VMEM((NT, 1, ROWS), f32),
            pltpu.VMEM((NT, 1, ROWS), f32),
            pltpu.VMEM((RANK, ROWS), f32),
            pltpu.SMEM((NG,), jnp.int32),
            pltpu.SemaphoreType.REGULAR, pltpu.SemaphoreType.REGULAR,
            dma, dma, dma((2,)), dma((3,)),
            dma((2,)), dma((2,)), dma((2,)), dma((2,)),
            dma, dma(((NY - 1) * CH,)), dma, dma((NY + 1,)),
            dma, dma, dma, dma,
        ],
        compiler_params=pltpu.CompilerParams(
            collective_id=0, has_side_effects=True, vmem_limit_bytes=VLIM * 1024),
        cost_estimate=pl.CostEstimate(flops=2 * ROWS * NT * KB * NB, bytes_accessed=8 << 20, transcendentals=0),
    )(*(pltpu.with_memory_space_constraint(x, pltpu.HBM) for x in (
        group_slot_adapters.T, adapter_storage_position, token_slot_index.reshape(1, ROWS),
        tokens, query_weight, down_weight, up_weight)))


def solution(mesh):
    in_specs = (
        P("group", "tensor"),
        P("group"),
        P(),
        P(),
        P(None, "tensor"),
        P(("group", "tensor"), None, None),
        P(("group", "tensor"), None, None),
    )
    return jax.shard_map(body, mesh=mesh, in_specs=in_specs, out_specs=P("group", "tensor"), check_vma=False)
```

```python
import functools

import jax
import jax.numpy as jnp
from jax import lax
from jax.experimental import pallas as pl
from jax.experimental.pallas import tpu as pltpu
from jax.sharding import PartitionSpec as P

RANK = 16
SLOTS = 16
SCALE = 0.5
NZ, NX, NY, NC = 8, 4, 8, 2
NG, NT = NZ * NX, NY * NC
ROWS = 512
KB = 512
NB = 256
CH = 4
CR = ROWS // CH
VLIM = 40 * 1024
PLUS = (0, 2)
MESH = pl.DeviceIdType.MESH


def kernel(
    gsa_hbm, asp_hbm, idx_hbm, tok, w_hbm, down, up, out_ref,
    gsa, asp, idx_ref, xall, w_v, down_panel, up_panel, down_staged, up_staged, down_inbox, up_inbox, down_slots, up_slots, acc, part, rs, lr, lr2, local_of, here, opened,
    w_sem, x_sem, own_sem, table_sem,
    ya_send, ya_recv, ga_send, ga_recv,
    ring_send, ring_recv, cross_send, cross_recv,
    rs_send, rs_recv, lr_send, lr_recv,
):
    g = lax.axis_index("group")
    t = lax.axis_index("tensor")
    y = t // NC
    c = t % NC
    other = y * NC + (1 - c)

    def tensor_peer(i):
        return lax.rem(t + NT + (2 * lax.rem(i, 2) - 1) * lax.div(i + 1, 2), NT)

    def group_peer(j):
        return lax.rem(g + NG + (2 * lax.rem(j, 2) - 1) * lax.div(j + 1, 2), NG)

    barrier = pltpu.get_barrier_semaphore()

    @pl.loop(1, NT)
    def _(i):
        dst = tensor_peer(i)

        @pl.when(dst != 0)
        def _():
            pl.semaphore_signal(barrier, inc=1, device_id={"group": g, "tensor": dst}, device_id_type=MESH)

    w_copy = pltpu.make_async_copy(w_hbm, w_v, w_sem)
    x_copy = pltpu.make_async_copy(tok, xall.at[t], x_sem)
    down_own = pltpu.make_async_copy(
        down.at[0, :, pl.ds(pl.multiple_of(t * KB, KB), KB)], down_panel.at[t], own_sem.at[0])
    up_own = pltpu.make_async_copy(
        up.at[0, :, pl.ds(pl.multiple_of(t * NB, NB), NB)], up_panel.at[t], own_sem.at[1])
    tables = [
        pltpu.make_async_copy(src, dst, table_sem.at[n])
        for n, (src, dst) in enumerate(((gsa_hbm, gsa), (asp_hbm, asp), (idx_hbm, idx_ref)))
    ]
    for copy in tables:
        copy.start()
    down_own.start()
    up_own.start()

    @pl.when(t != 0)
    def _():
        pl.semaphore_wait(barrier, NT - 1)

    @pl.when(t == 1)
    def _():
        pl.semaphore_signal(here, inc=1, device_id={"group": g, "tensor": t - 1}, device_id_type=MESH)

    @pl.when(t == 0)
    def _():
        pl.semaphore_wait(here, 1)

    def settled(block, send_sem, recv_sem):
        return pltpu.make_async_remote_copy(
            block, block, send_sem, recv_sem, device_id={"group": g, "tensor": other}, device_id_type=MESH)

    maps = (
        (down, KB, down_panel, down_staged, down_inbox, down_slots),
        (up, NB, up_panel, up_staged, up_inbox, up_slots),
    )

    def ya_copy(i, m):
        ref, width, panel = maps[m][:3]
        dst = tensor_peer(i)
        return pltpu.make_async_remote_copy(
            ref.at[0, :, pl.ds(pl.multiple_of(dst * width, width), width)], panel.at[t],
            ya_send.at[m], ya_recv.at[m], device_id={"group": g, "tensor": dst}, device_id_type=MESH)

    def ya_start(m):
        @pl.loop(1, NT)
        def _(i):
            ya_copy(i, m).start()

    def ya_all(m):
        return settled(maps[m][2].at[pl.ds(0, NT - 1)], ya_send.at[m], ya_recv.at[m])

    def ring_copy(src, block, d, k, way):
        dst_y = lax.rem(y + (1 if way == 0 else NY - 1), NY)
        rows = slice(k * CR, (k + 1) * CR)
        n = (d - 1) * 2 * CH + (2 * k + way if d < NY // 2 else k)
        return pltpu.make_async_remote_copy(
            src.at[rows, :], xall.at[block, rows, :], ring_send, ring_recv.at[n],
            device_id={"group": g, "tensor": dst_y * NC + c}, device_id_type=MESH)

    def cross_copy(src, block, h, k):
        rows = slice(k * CR, (k + 1) * CR)
        n = NY if h == NY // 2 and k >= CH // 2 else h
        return pltpu.make_async_remote_copy(
            src.at[rows, :], xall.at[block, rows, :], cross_send, cross_recv.at[n],
            device_id={"group": g, "tensor": other}, device_id_type=MESH)

    def cross_all(h):
        block = xall.at[0]
        if h in (NY // 2, NY):
            block = xall.at[0, pl.ds(0, ROWS // 2)]
        return settled(block, cross_send, cross_recv.at[h])

    def reaches(way, d, k):
        if d < NY // 2:
            return True
        return d == NY // 2 and (k in PLUS) == (way == 0)

    def source(way, d):
        ys = lax.rem(y + (NY - d if way == 0 else d), NY)
        return ys * NC + c, ys * NC + (1 - c)

    def own_sends():
        for k in range(CH):
            for way in (0, 1):
                ring_copy(tok, t, 1, k, way).start()
            cross_copy(tok, t, 0, k).start()

    def greet_groups():
        @pl.when(t == 0)
        def _():
            @pl.loop(1, NG)
            def _(j):
                pl.semaphore_signal(
                    barrier, inc=1, device_id={"group": group_peer(j), "tensor": t}, device_id_type=MESH)

    def pick_adapters():
        for copy in tables:
            copy.wait()

        @pl.loop(0, NG)
        def _(r):
            pick = jnp.int32(0)
            for s in range(SLOTS):
                place = asp[gsa[s, r]]
                pick = pick + jnp.where(lax.shift_right_logical(place, 4) == g, place & 15, 0)
            local_of[r] = pick

    def panel_wait(m):
        (down_own, up_own)[m].wait()

        ya_all(m).wait_recv()

    def groups_wait():
        @pl.when(t == 0)
        def _():
            pl.semaphore_wait(barrier, NG - 1)

            @pl.loop(1, NT)
            def _(i):
                pl.semaphore_signal(
                    opened, inc=1, device_id={"group": g, "tensor": tensor_peer(i)}, device_id_type=MESH)

        @pl.when(t != 0)
        def _():
            pl.semaphore_wait(opened, 1)

    def ga_copy(j, m):
        staged, inbox = maps[m][3:5]
        dst = group_peer(j)
        return pltpu.make_async_remote_copy(
            staged.at[j], inbox.at[g],
            ga_send.at[m], ga_recv.at[m], device_id={"group": dst, "tensor": t}, device_id_type=MESH)

    def send_adapters(m):
        panel, staged, inbox = maps[m][2:5]

        @pl.loop(1, NG)
        def _(j):
            staged[j] = panel[local_of[group_peer(j)]]
            ga_copy(j, m).start()

        inbox[g] = panel[local_of[g]]

    def ga_all(m):
        return settled(maps[m][4].at[pl.ds(0, NG - 1)], ga_send.at[m], ga_recv.at[m])

    def adapters_wait(m):
        inbox, slots = maps[m][4:]

        ga_all(m).wait_recv()

        for s in range(SLOTS):
            owner = lax.shift_right_logical(asp[gsa[s, g]], 4)
            slots[s * RANK:(s + 1) * RANK, :] = inbox[owner]

    def weight(block):
        return w_v[pl.ds(pl.multiple_of(block * KB, KB), KB), :]

    def accumulate(block, first=False):
        term = jnp.dot(xall[block], weight(block), preferred_element_type=jnp.float32)
        if first:
            acc[...] = term
        else:
            acc[...] += term

    def close(part_rows):
        far, far_other = source(0, NY // 2)
        rows = pl.ds(part_rows * (ROWS // 2), ROWS // 2)
        value = acc[rows, :] + jnp.dot(xall[far, rows, :], weight(far), preferred_element_type=jnp.float32)
        cross_all(NY if part_rows else NY // 2).wait_recv()
        value = value + jnp.dot(
            xall[far_other, rows, :], weight(far_other), preferred_element_type=jnp.float32)
        out_ref[rows, :] = value.astype(out_ref.dtype)

    def ring_step(d, ks=range(CH)):
        for k in ks:
            for way in (0, 1):
                if not reaches(way, d, k):
                    continue
                block, _ = source(way, d)
                ring_copy(xall.at[block], block, d, k, way).wait_recv()
                if reaches(way, d + 1, k):
                    ring_copy(xall.at[block], block, d + 1, k, way).start()
                h = d if way == 0 or d == NY // 2 else NY - d
                cross_copy(xall.at[block], block, h, k).start()

    def blocks_at(d):
        return (0,) if d == NY // 2 else (0, 1)

    def ring_own(d):
        if d == 0:
            accumulate(t, True)
            return
        for way in blocks_at(d):
            accumulate(source(way, d)[0])

    def ring_cross(d):
        for way in blocks_at(d) if d else (0,):
            h = d if way == 0 else NY - d
            block = source(way, d)[1]
            cross_all(h).wait_recv()
            accumulate(block)

    def rs_copy(i):
        dst = tensor_peer(i)
        return pltpu.make_async_remote_copy(
            part.at[dst], rs.at[t], rs_send, rs_recv,
            device_id={"group": g, "tensor": dst}, device_id_type=MESH)

    def rs_all():
        return settled(rs.at[pl.ds(0, NT - 1)], rs_send, rs_recv)

    def lr_all():
        return settled(lr.at[pl.ds(0, NT - 1)], lr_send, lr_recv)

    def lr_copy(i):
        return pltpu.make_async_remote_copy(
            lr.at[t], lr.at[t], lr_send, lr_recv,
            device_id={"group": g, "tensor": tensor_peer(i)}, device_id_type=MESH)

    def shrink():
        adapters_wait(0)
        idx = idx_ref[...]
        every = lax.dot_general(
            down_slots[...], xall[t], (((1,), (1,)), ((), ())), preferred_element_type=jnp.float32)
        partial = jnp.zeros((RANK, ROWS), jnp.float32)
        for s in range(SLOTS):
            partial = partial + jnp.where(idx == s, every[s * RANK:(s + 1) * RANK, :], 0.0)
        for r in range(RANK):
            part[r] = partial[r:r + 1, :]

        @pl.loop(1, NT)
        def _(i):
            rs_copy(i).start()

        rs[t] = part[t]

    def sum_shrink():
        rs_all().wait_recv()

        total = rs[0]
        for i in range(1, NT):
            total = total + rs[i]
        lr[t] = total

        @pl.loop(1, NT)
        def _(i):
            lr_copy(i).start()

    def early_sends():
        for m in (0, 1):
            ya_all(m).wait_send()
            ga_all(m).wait_send()
        rs_all().wait_send()

    def last_sends():
        lr_all().wait_send()
        settled(xall.at[pl.ds(0, NY - 1)], ring_send, ring_recv.at[0]).wait_send()
        settled(xall.at[pl.ds(0, NY)], cross_send, cross_recv.at[0]).wait_send()

    def expand():
        lr_all().wait_recv()

        for r in range(RANK):
            lr2[r:r + 1, :] = lr[r]
        low = lr2[...].astype(jnp.bfloat16).astype(jnp.float32)
        idx = idx_ref[...]
        spread = jnp.concatenate([jnp.where(idx == s, low, 0.0) for s in range(SLOTS)], axis=0)
        spread = jnp.transpose(spread).astype(jnp.bfloat16)
        adapter = jnp.dot(spread, up_slots[...], preferred_element_type=jnp.float32)
        acc[...] += SCALE * adapter

    def operands_wait():
        x_copy.wait()
        w_copy.wait()

    ya_start(0)
    own_sends()
    ya_start(1)
    x_copy.start()
    w_copy.start()
    greet_groups()
    pick_adapters()
    operands_wait()
    panel_wait(0)
    groups_wait()
    send_adapters(0)
    ring_own(0)
    ring_step(1)
    panel_wait(1)
    send_adapters(1)
    shrink()
    ring_step(2)
    ring_own(1)
    ring_cross(0)
    sum_shrink()
    ring_step(3)
    ring_own(2)
    ring_cross(1)
    early_sends()
    ring_cross(2)
    ring_own(3)
    ring_step(4, range(CH // 2))
    ring_cross(3)
    ring_step(4, range(CH // 2, CH))
    adapters_wait(1)
    expand()
    close(0)
    close(1)
    last_sends()


def body(tokens, token_slot_index, group_slot_adapters, adapter_storage_position, query_weight, down_weight, up_weight):
    hbm = pl.BlockSpec(memory_space=pltpu.HBM)
    vmem = pl.BlockSpec(memory_space=pltpu.VMEM)
    dma = pltpu.SemaphoreType.DMA
    bf16, f32 = jnp.bfloat16, jnp.float32
    return pl.pallas_call(
        kernel,
        out_shape=jax.ShapeDtypeStruct((ROWS, NB), bf16),
        in_specs=[hbm] * 7,
        out_specs=vmem,
        scratch_shapes=[
            pltpu.SMEM((SLOTS, NG), jnp.int32),
            pltpu.SMEM((NT * NG,), jnp.int32),
            pltpu.VMEM((1, ROWS), jnp.int32),
            pltpu.VMEM((NT, ROWS, KB), bf16),
            pltpu.VMEM((NT * KB, NB), bf16),
            pltpu.VMEM((NT, RANK, KB), bf16),
            pltpu.VMEM((NT, RANK, NB), bf16),
            pltpu.VMEM((NG, RANK, KB), bf16),
            pltpu.VMEM((NG, RANK, NB), bf16),
            pltpu.VMEM((NG, RANK, KB), bf16),
            pltpu.VMEM((NG, RANK, NB), bf16),
            pltpu.VMEM((SLOTS * RANK, KB), bf16),
            pltpu.VMEM((SLOTS * RANK, NB), bf16),
            pltpu.VMEM((ROWS, NB), f32),
            pltpu.VMEM((RANK, 1, ROWS), f32),
            pltpu.VMEM((NT, 1, ROWS), f32),
            pltpu.VMEM((NT, 1, ROWS), f32),
            pltpu.VMEM((RANK, ROWS), f32),
            pltpu.SMEM((NG,), jnp.int32),
            pltpu.SemaphoreType.REGULAR, pltpu.SemaphoreType.REGULAR,
            dma, dma, dma((2,)), dma((3,)),
            dma((2,)), dma((2,)), dma((2,)), dma((2,)),
            dma, dma(((NY - 1) * CH,)), dma, dma((NY + 1,)),
            dma, dma, dma, dma,
        ],
        compiler_params=pltpu.CompilerParams(
            collective_id=0, has_side_effects=True, vmem_limit_bytes=VLIM * 1024),
        cost_estimate=pl.CostEstimate(flops=2 * ROWS * NT * KB * NB, bytes_accessed=8 << 20, transcendentals=0),
    )(*(pltpu.with_memory_space_constraint(x, pltpu.HBM) for x in (
        group_slot_adapters.T, adapter_storage_position, token_slot_index.reshape(1, ROWS),
        tokens, query_weight, down_weight, up_weight)))


def solution(mesh):
    in_specs = (
        P("group", "tensor"),
        P("group"),
        P(),
        P(),
        P(None, "tensor"),
        P(("group", "tensor"), None, None),
        P(("group", "tensor"), None, None),
    )
    return jax.shard_map(body, mesh=mesh, in_specs=in_specs, out_specs=P("group", "tensor"), check_vma=False)
```
